512 devices in a mesh: section: 2 (over core), seq: 64 (over y, x, z_lo), mp: 4 (over z_hi).
Axes of the slice: x: 4, y: 4, z: 16 (z_hi: 4, z_lo: 4; z = z_hi * 4 + z_lo), core: 2. Of those that a mesh axis runs over, the one named last changes fastest.
Arguments:
- token_ids: int32 [2, 16384], P(None, 'seq'), may hold values from 0 to 511
- embed_table: bfloat16 [512, 4096], P(None, 'mp'), may hold values from -40 to 40
- norm_gain: bfloat16 [2, 4096], P('section', 'mp'), may hold values from 0.099609375 to 1.8984375
- short_filters: bfloat16 [2, 3, 7, 4096], P('section', None, None, 'mp'), may hold values from -2 to 2
- medium_filters: bfloat16 [2, 128, 4096], P('section', None, 'mp'), may hold values from -0.5 to 0.5
- out_weight: bfloat16 [2, 4096, 4096], P('section', 'seq', 'mp'), may hold values from -0.09375 to 0.09375
Outputs:
- streams: bfloat16 [2, 2, 16384, 4096], P('section', None, 'seq', 'mp')
The draws below stay inside these ranges and needn't reach their ends.
All inputs are finite; a program needn't handle non-finite values.
Results may differ from the reference program's by a relative error of at most 0.018.
Values may be sent and summed in bfloat16 or wider, within the bound.
No kernel may reach another device: no remote copies, remote signals or barrier semaphores. Data moves between devices by JAX's collectives and lax.ppermute only.
A program may use at most 64 MiB of HBM per device.

```python
import math
import jax
import jax.numpy as jnp
import numpy as np
from jax import lax

D = 4096
VOCAB = 512
SHORT_LEN = 7
MR_LEN = 128
MICRO = 2
SEQ_LEN = 16384
N_SECTION = 2


def draw_embed_table(key, part):
    base_key, row_key, col_key = jax.random.split(key, 3)
    base = jnp.clip(jax.random.normal(base_key, (VOCAB, D), jnp.float32), -4.0, 4.0)
    row_scale = jnp.exp(jax.random.uniform(row_key, (VOCAB, 1), jnp.float32, math.log(0.5), math.log(2.0)))
    col_scale = jnp.exp(jax.random.uniform(col_key, (1, D), jnp.float32, math.log(0.5), math.log(2.5)))
    ramp = 0.6 * jnp.exp(math.log(3.0) * jnp.arange(D, dtype=jnp.float32)[None, :] / D)
    return (base * row_scale * col_scale * ramp).astype(jnp.bfloat16)


def with_ends(array, own_key, least, high):
    longest = array.shape.index(max(array.shape))
    spots = []
    for shift in (0, 1):
        where = [jax.random.randint(jax.random.fold_in(own_key, axis), (), 0, length) for axis, length in enumerate(array.shape)]
        where[longest] = (where[longest] + shift) % array.shape[longest]
        spots.append(tuple(where))
    return array.at[spots[0]].set(least).at[spots[1]].set(high)


def level_of(stream_key, dims, shards, smallest, high):
    def one(position, parts):
        draws = jax.random.uniform(jax.random.fold_in(jax.random.fold_in(stream_key, 6), position), (parts,), jnp.float32, smallest / len(shards), high / len(shards))
        return jnp.repeat(jnp.exp(draws), dims[position] // parts).reshape((-1,) + (1,) * (len(dims) - position - 1))

    level = one(*shards[0])
    for cut in shards[1:]:
        level = level * one(*cut)
    return level


def cumulative_ranks(number_of, slope):
    weights = [(1 << 20) // math.isqrt(standing ** slope) + 1 for standing in range(1, number_of + 1)]
    deviation = 1 + sum(weights) // (1 << 30)
    return np.cumsum(np.array([max(1, weight // deviation) for weight in weights]))


def ranked(own_key, shape, count, slope):
    grid = cumulative_ranks(count, slope)
    lot = jax.random.randint(jax.random.fold_in(own_key, 1), shape, 0, int(grid[count - 1]))
    grade = jnp.searchsorted(jnp.asarray(grid, jnp.int32), lot, side="right")
    return jax.random.permutation(jax.random.fold_in(own_key, 2), count)[grade].astype(jnp.int32)


def centred(own_key, dims, scale, bound, cuts=(), held_as=jnp.bfloat16):
    loudness = level_of(own_key, dims, cuts, -0.22, 0.18) if cuts else 1.0
    array = jax.random.normal(own_key, dims, jnp.float32) * scale * loudness
    return jnp.minimum(jnp.maximum(array, -bound), bound).astype(held_as)


def setup_inputs(seed: int = 0) -> dict:
    keys = jax.random.split(jax.random.key(seed), 7)
    return {
        "token_ids": with_ends(ranked(keys[0], (MICRO, SEQ_LEN), VOCAB, 2), jax.random.fold_in(keys[0], 3), 0, VOCAB - 1).astype(jnp.int32),
        "embed_table": draw_embed_table(jax.random.fold_in(keys[6], 71), 0),
        "norm_gain": jnp.clip(1.0 + 0.18 * jax.random.normal(keys[2], (N_SECTION, D), jnp.float32), 0.099609375, 1.8984375).astype(jnp.bfloat16),
        "short_filters": centred(keys[3], (N_SECTION, 3, SHORT_LEN, D), SHORT_LEN ** -0.5, 2.0, ((0, 2), (3, 4))),
        "medium_filters": centred(keys[4], (N_SECTION, MR_LEN, D), MR_LEN ** -0.5, 0.5, ((0, 2), (2, 4))),
        "out_weight": centred(keys[5], (N_SECTION, D, D), D ** -0.5, 0.09375, ((0, 2), (1, 64), (2, 4))),
    }


def causal_filter(signal, taps):
    length = taps.shape[0]
    total_rows = signal.shape[0]
    padded = jnp.pad(signal.astype(jnp.float32), ((length - 1, 0), (0, 0)))
    taps_wide = taps.astype(jnp.float32)

    def add_tap(index, total):
        start = (length - 1 - index).astype(jnp.int32)
        window = lax.dynamic_slice_in_dim(padded, start, total_rows, 0)
        return total + taps_wide[index][None, :] * window
    initial = jnp.zeros((total_rows, signal.shape[1]), jnp.float32)
    return lax.fori_loop(jnp.int32(0), jnp.int32(length), add_tap, initial)

def mixer_layer(stream_in, gain, shorts, medium, weight):
    stream = stream_in.astype(jnp.float32)
    mean_square = lax.optimization_barrier(jnp.sum(stream * stream, axis=1, keepdims=True)) / D
    normed = (stream * lax.rsqrt(mean_square + 1e-06) * gain.astype(jnp.float32)[None, :]).astype(jnp.bfloat16)
    features = [causal_filter(normed, shorts[index]).astype(jnp.bfloat16) for index in range(3)]
    product = (features[1].astype(jnp.float32) * features[2].astype(jnp.float32)).astype(jnp.bfloat16)
    filtered = causal_filter(product, medium)
    gated = (features[0].astype(jnp.float32) * filtered).astype(jnp.bfloat16)
    projected = jnp.dot(gated, weight, preferred_element_type=jnp.float32)
    return (stream + projected).astype(jnp.bfloat16)

def reference(token_ids, embed_table, norm_gain, short_filters, medium_filters, out_weight):
    results = []
    for micro_index in range(MICRO):
        stream = embed_table[token_ids[micro_index]]
        per_section = []
        for section_index in range(N_SECTION):
            stream = mixer_layer(stream, norm_gain[section_index], short_filters[section_index], medium_filters[section_index], out_weight[section_index])
            per_section.append(stream)
        results.append(jnp.stack(per_section))
    return jnp.stack(results, axis=1)
```

```python
import itertools

import jax
import jax.numpy as jnp
from jax import lax
from jax.experimental import pallas as pl
from jax.experimental.pallas import tpu as pltpu
from jax.sharding import Mesh, PartitionSpec as P

D = 4096
ROWS = 256
HALF = 512
HALO = 144
REACH = 128
TILE = 128
MED = 128
PAR = 160
VOCAB = 512
F32 = jnp.float32
BF16 = jnp.bfloat16


STEPS = (0, 1, 3, 2)
LINES = (0, 2, 1, 3)


def ring(value, axis):
    return [value] + [lax.ppermute(value, axis, [((i + by) % 4, i) for i in range(4)]) for by in STEPS[1:]]


def in_order(pieces, position):
    one, two, three = pieces[1], pieces[3], pieces[2]
    twice = jnp.stack([pieces[0], one, two, three, pieces[0], one, two])
    return lax.dynamic_slice_in_dim(twice, (4 - position) % 4, 4, 0)


def other_core(value):
    return lax.ppermute(value, "s", [(0, 1), (1, 0)])


def permuted(value, axes, source):
    pairs = []
    for target in itertools.product(range(4), repeat=len(axes)):
        index = [0, 0]
        for a, b in zip(source(*target), target):
            index = [index[0] * 4 + a % 4, index[1] * 4 + b]
        pairs.append(tuple(index))
    return lax.ppermute(value, axes, pairs)


def channel_block(x, l, h):
    return (x + h + 2 * (l % 2)) % 4


def from_block(value, by):
    return permuted(value, ("x", "l", "h"), lambda x, l, h: (x + by, l, channel_block(x, l, h)))


def to_outputs_z(value):
    return permuted(value, ("x", "l", "h"), lambda x, l, h: (x, l, h - x - 2 * (l % 2)))


def to_outputs_x(value):
    return permuted(value, ("x", "l", "h"), lambda x, l, h: (h - x - 2 * (l % 2), l, h))


def working_tokens(value):
    return permuted(value, ("x", "h"), lambda x, h: (h, x))


def previous_block(value):
    def index(r):
        y, x, z = r // 64, r // 16 % 4, r % 16
        return ((y * 4 + x) * 4 + z % 4) * 4 + z // 4

    pairs = []
    for y, z, x in itertools.product(range(4), range(16), range(4)):
        r = 16 * y + z
        if r:
            yp, zp = divmod(r - 1, 16)
            c = channel_block(x, z % 4, z // 4)
            xp = (c - zp // 4 - 2 * (zp % 4 % 2)) % 4
            pairs.append((index(64 * yp + 16 * xp + zp), index(64 * y + 16 * x + z)))
    return lax.ppermute(value, ("y", "x", "l", "h"), pairs)


def previous_tokens(value):
    pairs = []
    for r in range(1, 64):
        y, z = divmod(r, 16)
        yp, zp = divmod(r - 1, 16)
        for x in range(4):
            source = ((yp * 4 + zp // 4) * 4 + zp % 4) * 4 + x
            target = ((y * 4 + x) * 4 + z % 4) * 4 + z // 4
            pairs.append((source, target))
    return lax.ppermute(value, ("y", "x", "l", "h"), pairs)


def filters(normed, par, shifted, product, query, gated):
    taps = [[par[MED + 7 * f + s : MED + 7 * f + s + 1, :] for s in range(7)] for f in range(3)]
    step = 64
    for c in range((REACH + ROWS) // step):
        first = HALO - REACH + c * step
        own = c * step >= REACH
        sums = [None] * 3
        for s in range(7):
            window = normed[first - s : first - s + step, :]
            for f in range(3):
                if f or own:
                    term = taps[f][s] * window
                    sums[f] = term if sums[f] is None else sums[f] + term
        key = sums[1].astype(BF16).astype(F32)
        value = sums[2].astype(BF16).astype(F32)
        product[c * step : (c + 1) * step, :] = (key * value).astype(BF16).astype(F32)
        if own:
            query[c * step - REACH : (c + 1) * step - REACH, :] = sums[0].astype(BF16).astype(F32)
    for j in range(8):
        shifted[j, 8 : REACH + ROWS, :] = product[8 - j : REACH + ROWS - j, :]
    block = 128
    for c in range(ROWS // block):

        def taps8(a, total):
            eight = par[pl.ds(pl.multiple_of(8 * a, 8), 8), :]
            start = pl.multiple_of(c * block + REACH - 8 * a, 8)
            for j in range(8):
                total = total + eight[j : j + 1, :] * shifted[j, pl.ds(start, block), :]
            return total

        total = lax.fori_loop(0, REACH // 8, taps8, jnp.zeros((block, TILE), F32))
        rows = slice(c * block, (c + 1) * block)
        gated[rows, :] = (query[rows, :] * total).astype(BF16)


def first_kernel(tokens, table, scale, par_in, gated, stream, par, normed, shifted, product, query):
    par[...] = par_in[...].astype(F32)
    gain = par[MED + 21 : MED + 22, :]
    entries = (table[...].astype(F32) * scale[...] * gain).astype(BF16)
    ids = lax.broadcasted_iota(jnp.int32, (HALO + ROWS, VOCAB), 1)
    chosen = jnp.where(tokens[0] == ids, 1.0, 0.0).astype(BF16)
    both = jnp.concatenate([entries, table[...]], axis=1)
    picked = jnp.dot(chosen, both, preferred_element_type=F32)
    normed[...] = picked[:, :TILE]
    stream[...] = picked[HALO:, TILE:].astype(BF16)
    filters(normed, par, shifted, product, query, gated)


def next_kernel(own, halo, scale, par_in, gated, par, normed, shifted, product, query):
    par[...] = par_in[...].astype(F32)
    gain = par[MED + 21 : MED + 22, :]
    normed[:HALO, :] = (halo[...].astype(F32) * scale[0, :HALO] * gain).astype(BF16).astype(F32)
    normed[HALO:, :] = (own[...].astype(F32) * scale[0, HALO:] * gain).astype(BF16).astype(F32)
    filters(normed, par, shifted, product, query, gated)


def filter_scratch():
    return [
        pltpu.VMEM((PAR, TILE), F32),
        pltpu.VMEM((HALO + ROWS, TILE), F32),
        pltpu.VMEM((8, REACH + ROWS, TILE), F32),
        pltpu.VMEM((REACH + ROWS, TILE), F32),
        pltpu.VMEM((ROWS, TILE), F32),
    ]


COST = pl.CostEstimate(flops=12_000_000_000, bytes_accessed=4_000_000, transcendentals=0)


def first_filters(tokens, table, scale, par):
    micros = tokens.shape[0]
    block = pl.BlockSpec((ROWS, TILE), lambda m, c: (m, c))
    return pl.pallas_call(
        first_kernel,
        grid=(micros, HALF // TILE),
        in_specs=[
            pl.BlockSpec((1, HALO + ROWS, 1), lambda m, c: (m, 0, 0)),
            pl.BlockSpec((VOCAB, TILE), lambda m, c: (0, c)),
            pl.BlockSpec((VOCAB, 1), lambda m, c: (0, 0)),
            pl.BlockSpec((PAR, TILE), lambda m, c: (0, c)),
        ],
        out_specs=[block, block],
        out_shape=[jax.ShapeDtypeStruct((micros * ROWS, HALF), BF16)] * 2,
        scratch_shapes=filter_scratch(),
        compiler_params=pltpu.CompilerParams(vmem_limit_bytes=32 * 1024 * 1024),
        cost_estimate=COST,
        name="first_filters",
    )(tokens, table, scale, par)


def next_filters(own, halo, scale, par):
    micros = scale.shape[0]
    return pl.pallas_call(
        next_kernel,
        grid=(micros, HALF // TILE),
        in_specs=[
            pl.BlockSpec((ROWS, TILE), lambda m, c: (m, c)),
            pl.BlockSpec((HALO, TILE), lambda m, c: (m, c)),
            pl.BlockSpec((1, HALO + ROWS, 1), lambda m, c: (m, 0, 0)),
            pl.BlockSpec((PAR, TILE), lambda m, c: (0, c)),
        ],
        out_specs=pl.BlockSpec((ROWS, TILE), lambda m, c: (m, c)),
        out_shape=jax.ShapeDtypeStruct((micros * ROWS, HALF), BF16),
        scratch_shapes=filter_scratch(),
        compiler_params=pltpu.CompilerParams(vmem_limit_bytes=32 * 1024 * 1024),
        cost_estimate=COST,
        name="next_filters",
    )(own, halo, scale, par)


def project_kernel(where, own, other, weights, stream, out, squares, whole, acts, sems, act_sems):
    s, c, l = where[0], where[1], where[2]
    copies = []
    for i in range(4):
        for j, flip in enumerate(LINES):
            copies.append(
                pltpu.make_async_copy(
                    weights.at[i, j], whole.at[i, :, lax.bitwise_xor(l, flip)], sems.at[i, j]
                )
            )
    copies.append(pltpu.make_async_copy(own, acts.at[0], act_sems.at[0]))
    copies.append(pltpu.make_async_copy(other, acts.at[1], act_sems.at[1]))
    for copy in copies:
        copy.start()
    for copy in copies:
        copy.wait()
    for m in range(stream.shape[0] // ROWS):
        rows = slice(m * ROWS, (m + 1) * ROWS)
        total = stream[rows, :].astype(F32)
        for i, step in enumerate(STEPS):
            for k in range(2):
                half = s if k == 0 else 1 - s
                w = whole[lax.rem(c + step, 4), pl.ds(2 * half, 2)].reshape(HALF, HALF)
                total = total + jnp.dot(acts[k, i, rows, :], w, preferred_element_type=F32)
        rounded = total.astype(BF16)
        out[rows, :] = rounded
        wide = rounded.astype(F32)
        squares[rows, :] = jnp.sum(wide * wide, axis=1, keepdims=True)


def project(where, acts, weights, stream):
    rows = stream.shape[0]
    vmem = pl.BlockSpec(memory_space=pltpu.VMEM)
    return pl.pallas_call(
        project_kernel,
        in_specs=[pl.BlockSpec(memory_space=pltpu.SMEM)] + [pl.BlockSpec(memory_space=pl.ANY)] * 3 + [vmem],
        out_specs=[vmem, vmem],
        out_shape=[
            jax.ShapeDtypeStruct((rows, HALF), BF16),
            jax.ShapeDtypeStruct((rows, 1), F32),
        ],
        scratch_shapes=[
            pltpu.VMEM((4, 4, 4, 64, HALF), BF16),
            pltpu.VMEM((2, 4, rows, HALF), BF16),
            pltpu.SemaphoreType.DMA((4, 4)),
            pltpu.SemaphoreType.DMA((2,)),
        ],
        compiler_params=pltpu.CompilerParams(vmem_limit_bytes=40 * 1024 * 1024),
        cost_estimate=pl.CostEstimate(flops=4_000_000_000, bytes_accessed=9_000_000, transcendentals=0),
        name="project",
    )(where, *acts, weights, stream)


def after(value, *others):
    return lax.optimization_barrier((value, *others))[0]


def gathered(gated):
    own = jnp.stack(ring(gated, "x"))
    return own, other_core(own)


def line_weights(shard):
    pieces = [
        shard,
        permuted(shard, ("l",), lambda l: (l ^ 2,)),
        permuted(shard, ("x", "l"), lambda x, l: (x + 2, l ^ 1)),
        permuted(shard, ("x", "l"), lambda x, l: (x + 2, l ^ 3)),
    ]
    return jnp.stack(pieces)


def local(token_ids, embed_table, norm_gain, short_filters, medium_filters, out_weight):
    s, y, x, l, h = (lax.axis_index(a) for a in ("s", "y", "x", "l", "h"))
    packed = jnp.concatenate(
        [medium_filters[0], short_filters[0].reshape(21, -1), norm_gain, jnp.zeros((10, 2 * HALF), BF16), out_weight[0]]
    )
    halves = packed[:, :HALF], packed[:, HALF:]
    mine = jnp.where(s == 0, halves[0], halves[1])
    theirs = other_core(jnp.where(s == 0, halves[1], halves[0]))
    layer_0 = jnp.where(s == 0, mine, theirs)
    layer_1 = jnp.where(s == 0, theirs, mine)
    own_ids = working_tokens(token_ids)
    before_ids = previous_tokens(token_ids[:, ROWS - HALO :])
    block_0 = (y == 0) & (l == 0) & (h == 0)
    before_ids = jnp.where(block_0, -1, before_ids)
    tokens = jnp.concatenate([before_ids, own_ids], axis=1)[:, :, None]
    wide = embed_table.astype(F32)
    partial = jnp.sum(wide * wide, axis=1).reshape(4, 128)
    entry_scale = lax.rsqrt(lax.psum(partial, "h") / D + 1e-06).reshape(VOCAB, 1)
    table_half = lax.dynamic_slice_in_dim(embed_table, s * HALF, HALF, 1)
    message = jnp.concatenate([table_half, layer_0[:PAR], jnp.zeros((32, HALF), BF16)])
    part = message.shape[0] // 4
    quarter = lax.dynamic_slice_in_dim(message, y * part, part, 0)
    raw = jnp.concatenate([layer_0[PAR:], layer_1[PAR:]])
    first = from_block(jnp.concatenate([quarter, raw]), 0)
    shards = in_order([first[part:]] + [from_block(raw, by) for by in STEPS[1:]], x).reshape(4, 2, 64, HALF)
    message = in_order(ring(first[:part], "y"), y).reshape(4 * part, HALF)
    table, par_0 = message[:VOCAB], message[VOCAB : VOCAB + PAR]
    where = jnp.stack([s, channel_block(x, l, h), l]).astype(jnp.int32)

    shards = after(shards, tokens, entry_scale)
    line_0 = line_weights(shards[:, 0])
    weights_0 = lax.all_gather(line_0, "y")
    gated, stream = first_filters(after(tokens, shards), table, entry_scale, par_0)
    acts = gathered(gated)
    line_1 = line_weights(after(shards[:, 1], gated))
    par_1 = from_block(after(layer_1[:PAR], gated), 0)
    stream_1, squares = project(where, acts, weights_0, after(stream, line_1))
    weights_1 = lax.all_gather(after(line_1, weights_0), "y")

    halo = previous_block(stream_1.reshape(2, ROWS, HALF)[:, ROWS - HALO :])
    squares = lax.psum(squares.reshape(4, 128), ("s", "x"))
    scale = lax.rsqrt(squares.reshape(2, ROWS) / D + 1e-06)
    scale = jnp.concatenate([previous_block(scale[:, ROWS - HALO :]), scale], axis=1)[:, :, None]
    result_0 = to_outputs_z(stream_1)
    gated = next_filters(stream_1, halo.reshape(2 * HALO, HALF), scale, par_1)
    acts = gathered(after(gated, result_0))
    result_0 = to_outputs_x(result_0)
    stream_2, _ = project(where, acts, weights_1, after(stream_1, result_0))
    result_1 = to_outputs_x(to_outputs_z(stream_2))

    kept = jnp.where(s == 0, result_0, result_1)
    received = other_core(jnp.where(s == 0, result_1, result_0))
    left = jnp.where(s == 0, kept, received)
    right = jnp.where(s == 0, received, kept)
    return jnp.concatenate([left, right], axis=1).reshape(1, 2, ROWS, 2 * HALF)


def solution(mesh):
    fine = Mesh(mesh.devices.reshape(2, 4, 4, 4, 4), ("s", "y", "x", "l", "h"))
    seq = ("y", "x", "l")
    in_specs = (
        P(None, seq),
        P(None, "h"),
        P("s", "h"),
        P("s", None, None, "h"),
        P("s", None, "h"),
        P("s", seq, "h"),
    )
    return jax.shard_map(local, mesh=fine, in_specs=in_specs, out_specs=P("s", None, seq, "h"), check_vma=False)
```

```python
import itertools

import jax
import jax.numpy as jnp
from jax import lax
from jax.experimental import pallas as pl
from jax.experimental.pallas import tpu as pltpu
from jax.sharding import Mesh, PartitionSpec as P

D = 4096
ROWS = 256
HALF = 512
HALO = 144
REACH = 128
TILE = 128
MED = 128
PAR = 160
VOCAB = 512
F32 = jnp.float32
BF16 = jnp.bfloat16


STEPS = (0, 1, 3, 2)
LINES = (0, 2, 1, 3)


def ring(value, axis):
    return [value] + [lax.ppermute(value, axis, [((i + by) % 4, i) for i in range(4)]) for by in STEPS[1:]]


def in_order(pieces, position):
    one, two, three = pieces[1], pieces[3], pieces[2]
    twice = jnp.stack([pieces[0], one, two, three, pieces[0], one, two])
    return lax.dynamic_slice_in_dim(twice, (4 - position) % 4, 4, 0)


def other_core(value):
    return lax.ppermute(value, "s", [(0, 1), (1, 0)])


def permuted(value, axes, source):
    pairs = []
    for target in itertools.product(range(4), repeat=len(axes)):
        index = [0, 0]
        for a, b in zip(source(*target), target):
            index = [index[0] * 4 + a % 4, index[1] * 4 + b]
        pairs.append(tuple(index))
    return lax.ppermute(value, axes, pairs)


def channel_block(x, l, h):
    return (x + h + 2 * (l % 2)) % 4


def from_block(value, by):
    return permuted(value, ("x", "l", "h"), lambda x, l, h: (x + by, l, channel_block(x, l, h)))


def to_outputs_z(value):
    return permuted(value, ("x", "l", "h"), lambda x, l, h: (x, l, h - x - 2 * (l % 2)))


def to_outputs_x(value):
    return permuted(value, ("x", "l", "h"), lambda x, l, h: (h - x - 2 * (l % 2), l, h))


def working_tokens(value):
    return permuted(value, ("x", "h"), lambda x, h: (h, x))


def previous_block(value):
    def index(r):
        y, x, z = r // 64, r // 16 % 4, r % 16
        return ((y * 4 + x) * 4 + z % 4) * 4 + z // 4

    pairs = []
    for y, z, x in itertools.product(range(4), range(16), range(4)):
        r = 16 * y + z
        if r:
            yp, zp = divmod(r - 1, 16)
            c = channel_block(x, z % 4, z // 4)
            xp = (c - zp // 4 - 2 * (zp % 4 % 2)) % 4
            pairs.append((index(64 * yp + 16 * xp + zp), index(64 * y + 16 * x + z)))
    return lax.ppermute(value, ("y", "x", "l", "h"), pairs)


def previous_tokens(value):
    pairs = []
    for r in range(1, 64):
        y, z = divmod(r, 16)
        yp, zp = divmod(r - 1, 16)
        for x in range(4):
            source = ((yp * 4 + zp // 4) * 4 + zp % 4) * 4 + x
            target = ((y * 4 + x) * 4 + z % 4) * 4 + z // 4
            pairs.append((source, target))
    return lax.ppermute(value, ("y", "x", "l", "h"), pairs)


def filters(normed, par, shifted, product, query, gated):
    taps = [[par[MED + 7 * f + s : MED + 7 * f + s + 1, :] for s in range(7)] for f in range(3)]
    step = 64
    for c in range((REACH + ROWS) // step):
        first = HALO - REACH + c * step
        own = c * step >= REACH
        sums = [None] * 3
        for s in range(7):
            window = normed[first - s : first - s + step, :]
            for f in range(3):
                if f or own:
                    term = taps[f][s] * window
                    sums[f] = term if sums[f] is None else sums[f] + term
        key = sums[1].astype(BF16).astype(F32)
        value = sums[2].astype(BF16).astype(F32)
        product[c * step : (c + 1) * step, :] = (key * value).astype(BF16).astype(F32)
        if own:
            query[c * step - REACH : (c + 1) * step - REACH, :] = sums[0].astype(BF16).astype(F32)
    for j in range(8):
        shifted[j, 8 : REACH + ROWS, :] = product[8 - j : REACH + ROWS - j, :]
    block = 128
    for c in range(ROWS // block):

        def taps8(a, total):
            eight = par[pl.ds(pl.multiple_of(8 * a, 8), 8), :]
            start = pl.multiple_of(c * block + REACH - 8 * a, 8)
            for j in range(8):
                total = total + eight[j : j + 1, :] * shifted[j, pl.ds(start, block), :]
            return total

        total = lax.fori_loop(0, REACH // 8, taps8, jnp.zeros((block, TILE), F32))
        rows = slice(c * block, (c + 1) * block)
        gated[rows, :] = (query[rows, :] * total).astype(BF16)


def first_kernel(tokens, table, scale, par_in, gated, stream, par, normed, shifted, product, query):
    par[...] = par_in[...].astype(F32)
    gain = par[MED + 21 : MED + 22, :]
    entries = (table[...].astype(F32) * scale[...] * gain).astype(BF16)
    ids = lax.broadcasted_iota(jnp.int32, (HALO + ROWS, VOCAB), 1)
    chosen = jnp.where(tokens[0] == ids, 1.0, 0.0).astype(BF16)
    both = jnp.concatenate([entries, table[...]], axis=1)
    picked = jnp.dot(chosen, both, preferred_element_type=F32)
    normed[...] = picked[:, :TILE]
    stream[...] = picked[HALO:, TILE:].astype(BF16)
    filters(normed, par, shifted, product, query, gated)


def next_kernel(own, halo, scale, par_in, gated, par, normed, shifted, product, query):
    par[...] = par_in[...].astype(F32)
    gain = par[MED + 21 : MED + 22, :]
    normed[:HALO, :] = (halo[...].astype(F32) * scale[0, :HALO] * gain).astype(BF16).astype(F32)
    normed[HALO:, :] = (own[...].astype(F32) * scale[0, HALO:] * gain).astype(BF16).astype(F32)
    filters(normed, par, shifted, product, query, gated)


def filter_scratch():
    return [
        pltpu.VMEM((PAR, TILE), F32),
        pltpu.VMEM((HALO + ROWS, TILE), F32),
        pltpu.VMEM((8, REACH + ROWS, TILE), F32),
        pltpu.VMEM((REACH + ROWS, TILE), F32),
        pltpu.VMEM((ROWS, TILE), F32),
    ]


SMALL = pl.CostEstimate(flops=1_000_000, bytes_accessed=1_000_000, transcendentals=0)
COST = pl.CostEstimate(flops=12_000_000_000, bytes_accessed=4_000_000, transcendentals=0)


def first_filters(tokens, table, scale, par):
    micros = tokens.shape[0]
    block = pl.BlockSpec((ROWS, TILE), lambda m, c: (m, c))
    return pl.pallas_call(
        first_kernel,
        grid=(micros, HALF // TILE),
        in_specs=[
            pl.BlockSpec((1, HALO + ROWS, 1), lambda m, c: (m, 0, 0)),
            pl.BlockSpec((VOCAB, TILE), lambda m, c: (0, c)),
            pl.BlockSpec((VOCAB, 1), lambda m, c: (0, 0)),
            pl.BlockSpec((PAR, TILE), lambda m, c: (0, c)),
        ],
        out_specs=[block, block],
        out_shape=[jax.ShapeDtypeStruct((micros * ROWS, HALF), BF16)] * 2,
        scratch_shapes=filter_scratch(),
        compiler_params=pltpu.CompilerParams(vmem_limit_bytes=32 * 1024 * 1024),
        cost_estimate=COST,
        name="first_filters",
    )(tokens, table, scale, par)


def next_filters(own, halo, scale, par):
    micros = scale.shape[0]
    return pl.pallas_call(
        next_kernel,
        grid=(micros, HALF // TILE),
        in_specs=[
            pl.BlockSpec((ROWS, TILE), lambda m, c: (m, c)),
            pl.BlockSpec((HALO, TILE), lambda m, c: (m, c)),
            pl.BlockSpec((1, HALO + ROWS, 1), lambda m, c: (m, 0, 0)),
            pl.BlockSpec((PAR, TILE), lambda m, c: (0, c)),
        ],
        out_specs=pl.BlockSpec((ROWS, TILE), lambda m, c: (m, c)),
        out_shape=jax.ShapeDtypeStruct((micros * ROWS, HALF), BF16),
        scratch_shapes=filter_scratch(),
        compiler_params=pltpu.CompilerParams(vmem_limit_bytes=32 * 1024 * 1024),
        cost_estimate=SMALL,
        name="next_filters",
    )(own, halo, scale, par)


def project_kernel(where, own, other, weights, stream, out, squares, whole, acts, sems, act_sems):
    s, c, l = where[0], where[1], where[2]
    copies = []
    for i in range(4):
        for j, flip in enumerate(LINES):
            copies.append(
                pltpu.make_async_copy(
                    weights.at[i, j], whole.at[i, :, lax.bitwise_xor(l, flip)], sems.at[i, j]
                )
            )
    copies.append(pltpu.make_async_copy(own, acts.at[0], act_sems.at[0]))
    copies.append(pltpu.make_async_copy(other, acts.at[1], act_sems.at[1]))
    for copy in copies:
        copy.start()
    for copy in copies:
        copy.wait()
    for m in range(stream.shape[0] // ROWS):
        rows = slice(m * ROWS, (m + 1) * ROWS)
        total = stream[rows, :].astype(F32)
        for i, step in enumerate(STEPS):
            for k in range(2):
                half = s if k == 0 else 1 - s
                w = whole[lax.rem(c + step, 4), pl.ds(2 * half, 2)].reshape(HALF, HALF)
                total = total + jnp.dot(acts[k, i, rows, :], w, preferred_element_type=F32)
        rounded = total.astype(BF16)
        out[rows, :] = rounded
        wide = rounded.astype(F32)
        squares[rows, :] = jnp.sum(wide * wide, axis=1, keepdims=True)


def project(where, acts, weights, stream):
    rows = stream.shape[0]
    vmem = pl.BlockSpec(memory_space=pltpu.VMEM)
    return pl.pallas_call(
        project_kernel,
        in_specs=[pl.BlockSpec(memory_space=pltpu.SMEM)] + [pl.BlockSpec(memory_space=pl.ANY)] * 2
        + [pl.BlockSpec(memory_space=pltpu.HBM), vmem],
        out_specs=[vmem, vmem],
        out_shape=[
            jax.ShapeDtypeStruct((rows, HALF), BF16),
            jax.ShapeDtypeStruct((rows, 1), F32),
        ],
        scratch_shapes=[
            pltpu.VMEM((4, 4, 4, 64, HALF), BF16),
            pltpu.VMEM((2, 4, rows, HALF), BF16),
            pltpu.SemaphoreType.DMA((4, 4)),
            pltpu.SemaphoreType.DMA((2,)),
        ],
        compiler_params=pltpu.CompilerParams(vmem_limit_bytes=40 * 1024 * 1024),
        cost_estimate=pl.CostEstimate(flops=4_000_000_000, bytes_accessed=9_000_000, transcendentals=0),
        name="project",
    )(where, *acts, weights, stream)


def after(value, *others):
    return lax.optimization_barrier((value, *others))[0]


def gathered(gated, *others):
    own = jnp.stack(ring(gated, "x"))
    return own, other_core(after(own, *others))


def line_weights(shard):
    pieces = [
        shard,
        permuted(shard, ("l",), lambda l: (l ^ 2,)),
        permuted(shard, ("x", "l"), lambda x, l: (x + 2, l ^ 1)),
        permuted(shard, ("x", "l"), lambda x, l: (x + 2, l ^ 3)),
    ]
    return jnp.stack(pieces)


def local(token_ids, embed_table, norm_gain, short_filters, medium_filters, out_weight):
    s, y, x, l, h = (lax.axis_index(a) for a in ("s", "y", "x", "l", "h"))
    packed = jnp.concatenate(
        [medium_filters[0], short_filters[0].reshape(21, -1), norm_gain, jnp.zeros((10, 2 * HALF), BF16), out_weight[0]]
    )
    halves = packed[:, :HALF], packed[:, HALF:]
    mine = jnp.where(s == 0, halves[0], halves[1])
    theirs = other_core(jnp.where(s == 0, halves[1], halves[0]))
    layer_0 = jnp.where(s == 0, mine, theirs)
    layer_1 = jnp.where(s == 0, theirs, mine)
    own_ids = working_tokens(token_ids)
    before_ids = previous_tokens(token_ids[:, ROWS - HALO :])
    block_0 = (y == 0) & (l == 0) & (h == 0)
    before_ids = jnp.where(block_0, -1, before_ids)
    tokens = jnp.concatenate([before_ids, own_ids], axis=1)[:, :, None]
    table_half = lax.dynamic_slice_in_dim(embed_table, s * HALF, HALF, 1)
    message = jnp.concatenate([table_half, layer_0[:PAR], layer_1[:PAR]])
    part = message.shape[0] // 4
    quarter = lax.dynamic_slice_in_dim(message, y * part, part, 0)
    raw = jnp.concatenate([layer_0[PAR:], layer_1[PAR:]])
    first = from_block(jnp.concatenate([quarter, raw]), 0)
    shards = in_order([first[part:]] + [from_block(raw, by) for by in STEPS[1:]], x).reshape(4, 2, 64, HALF)
    message = in_order(ring(first[:part], "y"), y).reshape(4 * part, HALF)
    table, par_0, par_1 = message[:VOCAB], message[VOCAB : VOCAB + PAR], message[VOCAB + PAR :]
    where = jnp.stack([s, channel_block(x, l, h), l]).astype(jnp.int32)

    wide = embed_table.astype(F32)
    partial = after(jnp.sum(wide * wide, axis=1).reshape(4, 128), first)
    entry_scale = lax.rsqrt(lax.psum(partial, "h") / D + 1e-06).reshape(VOCAB, 1)

    shards = after(shards, tokens, entry_scale)
    line_0 = line_weights(shards[:, 0])
    gated, stream = first_filters(after(tokens, shards), table, entry_scale, par_0)
    weights_0 = lax.all_gather(after(line_0, gated), "y")
    acts = gathered(gated)
    line_1 = line_weights(after(shards[:, 1], gated))
    stream_1, squares = project(where, acts, weights_0, after(stream, line_1))
    weights_1 = lax.all_gather(line_1, "y")

    halo = previous_block(stream_1.reshape(2, ROWS, HALF)[:, ROWS - HALO :])
    squares = lax.psum(squares.reshape(4, 128), ("s", "x"))
    scale = lax.rsqrt(squares.reshape(2, ROWS) / D + 1e-06)
    scale = jnp.concatenate([previous_block(scale[:, ROWS - HALO :]), scale], axis=1)[:, :, None]
    result_0a, result_0b = to_outputs_z(stream_1[:ROWS]), to_outputs_z(stream_1[ROWS:])
    gated = next_filters(after(stream_1, result_0a), halo.reshape(2 * HALO, HALF), scale, par_1)
    acts = gathered(gated, result_0b)
    stream_2, _ = project(where, acts, weights_1, stream_1)
    result_1 = to_outputs_x(to_outputs_z(stream_2))
    result_0 = to_outputs_x(jnp.concatenate([result_0a, result_0b]))

    kept = jnp.where(s == 0, result_0, result_1)
    received = other_core(jnp.where(s == 0, result_1, result_0))
    left = jnp.where(s == 0, kept, received)
    right = jnp.where(s == 0, received, kept)
    return jnp.concatenate([left, right], axis=1).reshape(1, 2, ROWS, 2 * HALF)


def solution(mesh):
    fine = Mesh(mesh.devices.reshape(2, 4, 4, 4, 4), ("s", "y", "x", "l", "h"))
    seq = ("y", "x", "l")
    in_specs = (
        P(None, seq),
        P(None, "h"),
        P("s", "h"),
        P("s", None, None, "h"),
        P("s", None, "h"),
        P("s", seq, "h"),
    )
    return jax.shard_map(local, mesh=fine, in_specs=in_specs, out_specs=P("s", None, seq, "h"), check_vma=False)
```

```python
import itertools

import jax
import jax.numpy as jnp
from jax import lax
from jax.experimental import pallas as pl
from jax.experimental.pallas import tpu as pltpu
from jax.sharding import Mesh, PartitionSpec as P

D = 4096
ROWS = 256
HALF = 512
HALO = 144
REACH = 128
TILE = 128
MED = 128
PAR = 160
VOCAB = 512
F32 = jnp.float32
BF16 = jnp.bfloat16


STEPS = (0, 1, 3, 2)
LINES = (0, 2, 1, 3)


def ring(value, axis):
    return [value] + [lax.ppermute(value, axis, [((i + by) % 4, i) for i in range(4)]) for by in STEPS[1:]]


def in_order(pieces, position):
    one, two, three = pieces[1], pieces[3], pieces[2]
    twice = jnp.stack([pieces[0], one, two, three, pieces[0], one, two])
    return lax.dynamic_slice_in_dim(twice, (4 - position) % 4, 4, 0)


def other_core(value):
    return lax.ppermute(value, "s", [(0, 1), (1, 0)])


def permuted(value, axes, source):
    pairs = []
    for target in itertools.product(range(4), repeat=len(axes)):
        index = [0, 0]
        for a, b in zip(source(*target), target):
            index = [index[0] * 4 + a % 4, index[1] * 4 + b]
        pairs.append(tuple(index))
    return lax.ppermute(value, axes, pairs)


def channel_block(x, l, h):
    return (x + h + l) % 4


def from_block(value, by):
    return permuted(value, ("x", "l", "h"), lambda x, l, h: (x + by, l, channel_block(x, l, h)))


def to_outputs_z(value):
    return permuted(value, ("x", "l", "h"), lambda x, l, h: (x, l, h - x - l))


def to_outputs_x(value):
    return permuted(value, ("x", "l", "h"), lambda x, l, h: (h - x - l, l, h))


def working_tokens(value):
    return permuted(value, ("x", "h"), lambda x, h: (h, x))


def previous_block(value):
    def index(r):
        y, x, z = r // 64, r // 16 % 4, r % 16
        return ((y * 4 + x) * 4 + z % 4) * 4 + z // 4

    pairs = []
    for y, z, x in itertools.product(range(4), range(16), range(4)):
        r = 16 * y + z
        if r:
            yp, zp = divmod(r - 1, 16)
            c = channel_block(x, z % 4, z // 4)
            xp = (c - zp // 4 - zp % 4) % 4
            pairs.append((index(64 * yp + 16 * xp + zp), index(64 * y + 16 * x + z)))
    return lax.ppermute(value, ("y", "x", "l", "h"), pairs)


def previous_tokens(value):
    pairs = []
    for r in range(1, 64):
        y, z = divmod(r, 16)
        yp, zp = divmod(r - 1, 16)
        for x in range(4):
            source = ((yp * 4 + zp // 4) * 4 + zp % 4) * 4 + x
            target = ((y * 4 + x) * 4 + z % 4) * 4 + z // 4
            pairs.append((source, target))
    return lax.ppermute(value, ("y", "x", "l", "h"), pairs)


def filters(normed, par, shifted, product, query, gated):
    taps = [[par[MED + 7 * f + s : MED + 7 * f + s + 1, :] for s in range(7)] for f in range(3)]
    step = 64
    for c in range((REACH + ROWS) // step):
        first = HALO - REACH + c * step
        own = c * step >= REACH
        sums = [None] * 3
        for s in range(7):
            window = normed[first - s : first - s + step, :]
            for f in range(3):
                if f or own:
                    term = taps[f][s] * window
                    sums[f] = term if sums[f] is None else sums[f] + term
        key = sums[1].astype(BF16).astype(F32)
        value = sums[2].astype(BF16).astype(F32)
        product[c * step : (c + 1) * step, :] = (key * value).astype(BF16).astype(F32)
        if own:
            query[c * step - REACH : (c + 1) * step - REACH, :] = sums[0].astype(BF16).astype(F32)
    for j in range(8):
        shifted[j, 8 : REACH + ROWS, :] = product[8 - j : REACH + ROWS - j, :]
    block = 128
    for c in range(ROWS // block):

        def taps8(a, total):
            eight = par[pl.ds(pl.multiple_of(8 * a, 8), 8), :]
            start = pl.multiple_of(c * block + REACH - 8 * a, 8)
            for j in range(8):
                total = total + eight[j : j + 1, :] * shifted[j, pl.ds(start, block), :]
            return total

        total = lax.fori_loop(0, REACH // 8, taps8, jnp.zeros((block, TILE), F32))
        rows = slice(c * block, (c + 1) * block)
        gated[rows, :] = (query[rows, :] * total).astype(BF16)


def first_kernel(tokens, table, scale, par_in, gated, stream, par, normed, shifted, product, query):
    par[...] = par_in[...].astype(F32)
    gain = par[MED + 21 : MED + 22, :]
    entries = (table[...].astype(F32) * scale[...] * gain).astype(BF16)
    ids = lax.broadcasted_iota(jnp.int32, (HALO + ROWS, VOCAB), 1)
    chosen = jnp.where(tokens[0] == ids, 1.0, 0.0).astype(BF16)
    both = jnp.concatenate([entries, table[...]], axis=1)
    picked = jnp.dot(chosen, both, preferred_element_type=F32)
    normed[...] = picked[:, :TILE]
    stream[...] = picked[HALO:, TILE:].astype(BF16)
    filters(normed, par, shifted, product, query, gated)


def next_kernel(own, halo, scale, par_in, gated, par, normed, shifted, product, query):
    par[...] = par_in[...].astype(F32)
    gain = par[MED + 21 : MED + 22, :]
    normed[:HALO, :] = (halo[...].astype(F32) * scale[0, :HALO] * gain).astype(BF16).astype(F32)
    normed[HALO:, :] = (own[...].astype(F32) * scale[0, HALO:] * gain).astype(BF16).astype(F32)
    filters(normed, par, shifted, product, query, gated)


def filter_scratch():
    return [
        pltpu.VMEM((PAR, TILE), F32),
        pltpu.VMEM((HALO + ROWS, TILE), F32),
        pltpu.VMEM((8, REACH + ROWS, TILE), F32),
        pltpu.VMEM((REACH + ROWS, TILE), F32),
        pltpu.VMEM((ROWS, TILE), F32),
    ]


SMALL = pl.CostEstimate(flops=1_000_000, bytes_accessed=1_000_000, transcendentals=0)
COST = pl.CostEstimate(flops=12_000_000_000, bytes_accessed=4_000_000, transcendentals=0)


def first_filters(tokens, table, scale, par):
    micros = tokens.shape[0]
    block = pl.BlockSpec((ROWS, TILE), lambda m, c: (m, c))
    return pl.pallas_call(
        first_kernel,
        grid=(micros, HALF // TILE),
        in_specs=[
            pl.BlockSpec((1, HALO + ROWS, 1), lambda m, c: (m, 0, 0)),
            pl.BlockSpec((VOCAB, TILE), lambda m, c: (0, c)),
            pl.BlockSpec((VOCAB, 1), lambda m, c: (0, 0)),
            pl.BlockSpec((PAR, TILE), lambda m, c: (0, c)),
        ],
        out_specs=[block, block],
        out_shape=[jax.ShapeDtypeStruct((micros * ROWS, HALF), BF16)] * 2,
        scratch_shapes=filter_scratch(),
        compiler_params=pltpu.CompilerParams(vmem_limit_bytes=32 * 1024 * 1024),
        cost_estimate=COST,
        name="first_filters",
    )(tokens, table, scale, par)


def next_filters(own, halo, scale, par):
    micros = scale.shape[0]
    return pl.pallas_call(
        next_kernel,
        grid=(micros, HALF // TILE),
        in_specs=[
            pl.BlockSpec((ROWS, TILE), lambda m, c: (m, c)),
            pl.BlockSpec((HALO, TILE), lambda m, c: (m, c)),
            pl.BlockSpec((1, HALO + ROWS, 1), lambda m, c: (m, 0, 0)),
            pl.BlockSpec((PAR, TILE), lambda m, c: (0, c)),
        ],
        out_specs=pl.BlockSpec((ROWS, TILE), lambda m, c: (m, c)),
        out_shape=jax.ShapeDtypeStruct((micros * ROWS, HALF), BF16),
        scratch_shapes=filter_scratch(),
        compiler_params=pltpu.CompilerParams(vmem_limit_bytes=32 * 1024 * 1024),
        cost_estimate=SMALL,
        name="next_filters",
    )(own, halo, scale, par)


def project_kernel(where, own, other, weights, stream, out, squares, whole, acts, sems, act_sems):
    s, c, l = where[0], where[1], where[2]
    copies = []
    for i in range(4):
        for j, flip in enumerate(LINES):
            copies.append(
                pltpu.make_async_copy(
                    weights.at[i, j], whole.at[i, :, lax.bitwise_xor(l, flip)], sems.at[i, j]
                )
            )
    copies.append(pltpu.make_async_copy(own, acts.at[0], act_sems.at[0]))
    copies.append(pltpu.make_async_copy(other, acts.at[1], act_sems.at[1]))
    for copy in copies:
        copy.start()
    for copy in copies:
        copy.wait()
    for m in range(stream.shape[0] // ROWS):
        rows = slice(m * ROWS, (m + 1) * ROWS)
        total = stream[rows, :].astype(F32)
        for i, step in enumerate(STEPS):
            for k in range(2):
                half = s if k == 0 else 1 - s
                w = whole[lax.rem(c + step, 4), pl.ds(2 * half, 2)].reshape(HALF, HALF)
                total = total + jnp.dot(acts[k, i, rows, :], w, preferred_element_type=F32)
        rounded = total.astype(BF16)
        out[rows, :] = rounded
        wide = rounded.astype(F32)
        squares[rows, :] = jnp.sum(wide * wide, axis=1, keepdims=True)


def project(where, acts, weights, stream):
    rows = stream.shape[0]
    vmem = pl.BlockSpec(memory_space=pltpu.VMEM)
    return pl.pallas_call(
        project_kernel,
        in_specs=[pl.BlockSpec(memory_space=pltpu.SMEM)] + [pl.BlockSpec(memory_space=pltpu.HBM)] * 3 + [vmem],
        out_specs=[vmem, vmem],
        out_shape=[
            jax.ShapeDtypeStruct((rows, HALF), BF16),
            jax.ShapeDtypeStruct((rows, 1), F32),
        ],
        scratch_shapes=[
            pltpu.VMEM((4, 4, 4, 64, HALF), BF16),
            pltpu.VMEM((2, 4, rows, HALF), BF16),
            pltpu.SemaphoreType.DMA((4, 4)),
            pltpu.SemaphoreType.DMA((2,)),
        ],
        compiler_params=pltpu.CompilerParams(vmem_limit_bytes=40 * 1024 * 1024),
        cost_estimate=pl.CostEstimate(flops=4_000_000_000, bytes_accessed=9_000_000, transcendentals=0),
        name="project",
    )(where, *acts, weights, stream)


def after(value, *others):
    return lax.optimization_barrier((value, *others))[0]


def gathered(gated, *others):
    own = jnp.stack(ring(gated, "x"))
    return own, other_core(after(own, *others))


def line_weights(shard):
    pieces = [shard]
    for flip in LINES[1:]:
        pieces.append(permuted(shard, ("x", "l"), lambda x, l, flip=flip: (x + l - (l ^ flip), l ^ flip)))
    return jnp.stack(pieces)


def local(token_ids, embed_table, norm_gain, short_filters, medium_filters, out_weight):
    s, y, x, l, h = (lax.axis_index(a) for a in ("s", "y", "x", "l", "h"))
    packed = jnp.concatenate(
        [medium_filters[0], short_filters[0].reshape(21, -1), norm_gain, jnp.zeros((10, 2 * HALF), BF16), out_weight[0]]
    )
    halves = packed[:, :HALF], packed[:, HALF:]
    mine = jnp.where(s == 0, halves[0], halves[1])
    theirs = other_core(jnp.where(s == 0, halves[1], halves[0]))
    layer_0 = jnp.where(s == 0, mine, theirs)
    layer_1 = jnp.where(s == 0, theirs, mine)
    own_ids = working_tokens(token_ids)
    before_ids = previous_tokens(token_ids[:, ROWS - HALO :])
    block_0 = (y == 0) & (l == 0) & (h == 0)
    before_ids = jnp.where(block_0, -1, before_ids)
    tokens = jnp.concatenate([before_ids, own_ids], axis=1)[:, :, None]
    table_half = lax.dynamic_slice_in_dim(embed_table, s * HALF, HALF, 1)
    message = jnp.concatenate([table_half, layer_0[:PAR], layer_1[:PAR]])
    part = message.shape[0] // 4
    quarter = lax.dynamic_slice_in_dim(message, y * part, part, 0)
    raw = jnp.concatenate([layer_0[PAR:], layer_1[PAR:]])
    first = from_block(jnp.concatenate([quarter, raw]), 0)
    shards = in_order([first[part:]] + [from_block(raw, by) for by in STEPS[1:]], x).reshape(4, 2, 64, HALF)
    message = in_order(ring(first[:part], "y"), y).reshape(4 * part, HALF)
    table, par_0, par_1 = message[:VOCAB], message[VOCAB : VOCAB + PAR], message[VOCAB + PAR :]
    where = jnp.stack([s, channel_block(x, l, h), l]).astype(jnp.int32)

    wide = embed_table.astype(F32)
    partial = after(jnp.sum(wide * wide, axis=1).reshape(4, 128), first)
    entry_scale = lax.rsqrt(sum(ring(partial, "h")) / D + 1e-06).reshape(VOCAB, 1)

    shards = after(shards, tokens, entry_scale)
    line_0 = line_weights(shards[:, 0])
    gated, stream = first_filters(after(tokens, shards), table, entry_scale, par_0)
    weights_0 = lax.all_gather(after(line_0, gated), "y")
    acts = gathered(gated)
    line_1 = line_weights(after(shards[:, 1], gated))
    stream_1, squares = project(where, acts, weights_0, after(stream, line_1))
    weights_1 = lax.all_gather(line_1, "y")

    halo = previous_block(stream_1.reshape(2, ROWS, HALF)[:, ROWS - HALO :])
    squares = lax.psum(squares.reshape(4, 128), ("s", "x"))
    scale = lax.rsqrt(squares.reshape(2, ROWS) / D + 1e-06)
    scale = jnp.concatenate([previous_block(scale[:, ROWS - HALO :]), scale], axis=1)[:, :, None]
    result_0a, result_0b = to_outputs_z(stream_1[:ROWS]), to_outputs_z(stream_1[ROWS:])
    gated = next_filters(after(stream_1, result_0a), halo.reshape(2 * HALO, HALF), scale, par_1)
    acts = gathered(gated, result_0b)
    stream_2, _ = project(where, acts, weights_1, stream_1)
    result_1 = to_outputs_x(to_outputs_z(stream_2))
    result_0 = to_outputs_x(jnp.concatenate([result_0a, result_0b]))

    kept = jnp.where(s == 0, result_0, result_1)
    received = other_core(jnp.where(s == 0, result_1, result_0))
    left = jnp.where(s == 0, kept, received)
    right = jnp.where(s == 0, received, kept)
    return jnp.concatenate([left, right], axis=1).reshape(1, 2, ROWS, 2 * HALF)


def solution(mesh):
    fine = Mesh(mesh.devices.reshape(2, 4, 4, 4, 4), ("s", "y", "x", "l", "h"))
    seq = ("y", "x", "l")
    in_specs = (
        P(None, seq),
        P(None, "h"),
        P("s", "h"),
        P("s", None, None, "h"),
        P("s", None, "h"),
        P("s", seq, "h"),
    )
    return jax.shard_map(local, mesh=fine, in_specs=in_specs, out_specs=P("s", None, seq, "h"), check_vma=False)
```

```python
import itertools

import jax
import jax.numpy as jnp
from jax import lax
from jax.experimental import pallas as pl
from jax.experimental.pallas import tpu as pltpu
from jax.sharding import Mesh, PartitionSpec as P

D = 4096
ROWS = 256
HALF = 512
HALO = 144
REACH = 128
TILE = 128
MED = 128
PAR = 160
VOCAB = 512
F32 = jnp.float32
BF16 = jnp.bfloat16


STEPS = (0, 1, 3, 2)
LINES = (0, 2, 1, 3)


def ring(value, axis):
    return [value] + [lax.ppermute(value, axis, [((i + by) % 4, i) for i in range(4)]) for by in STEPS[1:]]


def in_order(pieces, position):
    one, two, three = pieces[1], pieces[3], pieces[2]
    twice = jnp.stack([pieces[0], one, two, three, pieces[0], one, two])
    return lax.dynamic_slice_in_dim(twice, (4 - position) % 4, 4, 0)


def other_core(value):
    return lax.ppermute(value, "s", [(0, 1), (1, 0)])


def permuted(value, axes, source):
    pairs = []
    for target in itertools.product(range(4), repeat=len(axes)):
        index = [0, 0]
        for a, b in zip(source(*target), target):
            index = [index[0] * 4 + a % 4, index[1] * 4 + b]
        pairs.append(tuple(index))
    return lax.ppermute(value, axes, pairs)


def channel_block(x, l, h):
    return (x + h + l) % 4


def from_block(value, by):
    return permuted(value, ("x", "l", "h"), lambda x, l, h: (x + by, l, channel_block(x, l, h)))


def to_outputs_z(value):
    return permuted(value, ("x", "l", "h"), lambda x, l, h: (x, l, h - x - l))


def to_outputs_x(value):
    return permuted(value, ("x", "l", "h"), lambda x, l, h: (h - x - l, l, h))


def working_tokens(value):
    return permuted(value, ("x", "h"), lambda x, h: (h, x))


def previous_block(value):
    def index(r):
        y, x, z = r // 64, r // 16 % 4, r % 16
        return ((y * 4 + x) * 4 + z % 4) * 4 + z // 4

    pairs = []
    for y, z, x in itertools.product(range(4), range(16), range(4)):
        r = 16 * y + z
        if r:
            yp, zp = divmod(r - 1, 16)
            c = channel_block(x, z % 4, z // 4)
            xp = (c - zp // 4 - zp % 4) % 4
            pairs.append((index(64 * yp + 16 * xp + zp), index(64 * y + 16 * x + z)))
    return lax.ppermute(value, ("y", "x", "l", "h"), pairs)


def previous_tokens(value):
    pairs = []
    for r in range(1, 64):
        y, z = divmod(r, 16)
        yp, zp = divmod(r - 1, 16)
        for x in range(4):
            source = ((yp * 4 + zp // 4) * 4 + zp % 4) * 4 + x
            target = ((y * 4 + x) * 4 + z % 4) * 4 + z // 4
            pairs.append((source, target))
    return lax.ppermute(value, ("y", "x", "l", "h"), pairs)


def filters(normed, par, shifted, product, query, gated):
    taps = [[par[MED + 7 * f + s : MED + 7 * f + s + 1, :] for s in range(7)] for f in range(3)]
    step = 64
    for c in range((REACH + ROWS) // step):
        first = HALO - REACH + c * step
        own = c * step >= REACH
        sums = [None] * 3
        for s in range(7):
            window = normed[first - s : first - s + step, :]
            for f in range(3):
                if f or own:
                    term = taps[f][s] * window
                    sums[f] = term if sums[f] is None else sums[f] + term
        key = sums[1].astype(BF16).astype(F32)
        value = sums[2].astype(BF16).astype(F32)
        product[c * step : (c + 1) * step, :] = (key * value).astype(BF16).astype(F32)
        if own:
            query[c * step - REACH : (c + 1) * step - REACH, :] = sums[0].astype(BF16).astype(F32)
    for j in range(8):
        shifted[j, 8 : REACH + ROWS, :] = product[8 - j : REACH + ROWS - j, :]
    block = 128
    for c in range(ROWS // block):

        def taps8(a, total):
            eight = par[pl.ds(pl.multiple_of(8 * a, 8), 8), :]
            start = pl.multiple_of(c * block + REACH - 8 * a, 8)
            for j in range(8):
                total = total + eight[j : j + 1, :] * shifted[j, pl.ds(start, block), :]
            return total

        total = lax.fori_loop(0, REACH // 8, taps8, jnp.zeros((block, TILE), F32))
        rows = slice(c * block, (c + 1) * block)
        gated[rows, :] = (query[rows, :] * total).astype(BF16)


def first_kernel(tokens, table, scale, par_in, gated, stream, par, normed, shifted, product, query):
    par[...] = par_in[...].astype(F32)
    gain = par[MED + 21 : MED + 22, :]
    entries = (table[...].astype(F32) * scale[...] * gain).astype(BF16)
    ids = lax.broadcasted_iota(jnp.int32, (HALO + ROWS, VOCAB), 1)
    chosen = jnp.where(tokens[0] == ids, 1.0, 0.0).astype(BF16)
    both = jnp.concatenate([entries, table[...]], axis=1)
    picked = jnp.dot(chosen, both, preferred_element_type=F32)
    normed[...] = picked[:, :TILE]
    stream[...] = picked[HALO:, TILE:].astype(BF16)
    filters(normed, par, shifted, product, query, gated)


def next_kernel(own, halo, scale, par_in, gated, par, normed, shifted, product, query):
    par[...] = par_in[...].astype(F32)
    gain = par[MED + 21 : MED + 22, :]
    normed[:HALO, :] = (halo[...].astype(F32) * scale[0, :HALO] * gain).astype(BF16).astype(F32)
    normed[HALO:, :] = (own[...].astype(F32) * scale[0, HALO:] * gain).astype(BF16).astype(F32)
    filters(normed, par, shifted, product, query, gated)


def filter_scratch():
    return [
        pltpu.VMEM((PAR, TILE), F32),
        pltpu.VMEM((HALO + ROWS, TILE), F32),
        pltpu.VMEM((8, REACH + ROWS, TILE), F32),
        pltpu.VMEM((REACH + ROWS, TILE), F32),
        pltpu.VMEM((ROWS, TILE), F32),
    ]


SMALL = pl.CostEstimate(flops=1_000_000, bytes_accessed=1_000_000, transcendentals=0)
COST = pl.CostEstimate(flops=12_000_000_000, bytes_accessed=4_000_000, transcendentals=0)


def first_filters(tokens, table, scale, par):
    micros = tokens.shape[0]
    block = pl.BlockSpec((ROWS, TILE), lambda m, c: (m, c))
    return pl.pallas_call(
        first_kernel,
        grid=(micros, HALF // TILE),
        in_specs=[
            pl.BlockSpec((1, HALO + ROWS, 1), lambda m, c: (m, 0, 0)),
            pl.BlockSpec((VOCAB, TILE), lambda m, c: (0, c)),
            pl.BlockSpec((VOCAB, 1), lambda m, c: (0, 0)),
            pl.BlockSpec((PAR, TILE), lambda m, c: (0, c)),
        ],
        out_specs=[block, block],
        out_shape=[jax.ShapeDtypeStruct((micros * ROWS, HALF), BF16)] * 2,
        scratch_shapes=filter_scratch(),
        compiler_params=pltpu.CompilerParams(vmem_limit_bytes=32 * 1024 * 1024),
        cost_estimate=COST,
        name="first_filters",
    )(tokens, table, scale, par)


def next_filters(own, halo, scale, par):
    micros = scale.shape[0]
    return pl.pallas_call(
        next_kernel,
        grid=(micros, HALF // TILE),
        in_specs=[
            pl.BlockSpec((ROWS, TILE), lambda m, c: (m, c)),
            pl.BlockSpec((HALO, TILE), lambda m, c: (m, c)),
            pl.BlockSpec((1, HALO + ROWS, 1), lambda m, c: (m, 0, 0)),
            pl.BlockSpec((PAR, TILE), lambda m, c: (0, c)),
        ],
        out_specs=pl.BlockSpec((ROWS, TILE), lambda m, c: (m, c)),
        out_shape=jax.ShapeDtypeStruct((micros * ROWS, HALF), BF16),
        scratch_shapes=filter_scratch(),
        compiler_params=pltpu.CompilerParams(vmem_limit_bytes=32 * 1024 * 1024),
        cost_estimate=SMALL,
        name="next_filters",
    )(own, halo, scale, par)


def project_kernel(where, own, other, weights, stream, out, squares, whole, acts, sems, act_sems):
    s, c, l = where[0], where[1], where[2]
    copies = []
    for i in range(4):
        for j, flip in enumerate(LINES):
            copies.append(
                pltpu.make_async_copy(
                    weights.at[i, j], whole.at[i, :, lax.bitwise_xor(l, flip)], sems.at[i, j]
                )
            )
    copies.append(pltpu.make_async_copy(own, acts.at[0], act_sems.at[0]))
    copies.append(pltpu.make_async_copy(other, acts.at[1], act_sems.at[1]))
    for copy in copies:
        copy.start()
    for copy in copies:
        copy.wait()
    for m in range(stream.shape[0] // ROWS):
        rows = slice(m * ROWS, (m + 1) * ROWS)
        total = stream[rows, :].astype(F32)
        for i, step in enumerate(STEPS):
            for k in range(2):
                half = s if k == 0 else 1 - s
                w = whole[lax.rem(c + step, 4), pl.ds(2 * half, 2)].reshape(HALF, HALF)
                total = total + jnp.dot(acts[k, i, rows, :], w, preferred_element_type=F32)
        rounded = total.astype(BF16)
        out[rows, :] = rounded
        wide = rounded.astype(F32)
        squares[rows, :] = jnp.sum(wide * wide, axis=1, keepdims=True)


def project(where, acts, weights, stream):
    rows = stream.shape[0]
    vmem = pl.BlockSpec(memory_space=pltpu.VMEM)
    return pl.pallas_call(
        project_kernel,
        in_specs=[pl.BlockSpec(memory_space=pltpu.SMEM)] + [pl.BlockSpec(memory_space=pltpu.HBM)] * 3 + [vmem],
        out_specs=[vmem, vmem],
        out_shape=[
            jax.ShapeDtypeStruct((rows, HALF), BF16),
            jax.ShapeDtypeStruct((rows, 1), F32),
        ],
        scratch_shapes=[
            pltpu.VMEM((4, 4, 4, 64, HALF), BF16),
            pltpu.VMEM((2, 4, rows, HALF), BF16),
            pltpu.SemaphoreType.DMA((4, 4)),
            pltpu.SemaphoreType.DMA((2,)),
        ],
        compiler_params=pltpu.CompilerParams(vmem_limit_bytes=40 * 1024 * 1024),
        cost_estimate=pl.CostEstimate(flops=4_000_000_000, bytes_accessed=9_000_000, transcendentals=0),
        name="project",
    )(where, *acts, weights, stream)


def after(value, *others):
    return lax.optimization_barrier((value, *others))[0]


def gathered(gated, *others):
    own = jnp.stack(ring(gated, "x"))
    return own, other_core(after(own, *others))


def line_weights(shard):
    pieces = [shard]
    for flip in LINES[1:]:
        pieces.append(permuted(shard, ("x", "l"), lambda x, l, flip=flip: (x + l - (l ^ flip), l ^ flip)))
    return jnp.stack(pieces)


def local(token_ids, embed_table, norm_gain, short_filters, medium_filters, out_weight):
    s, y, x, l, h = (lax.axis_index(a) for a in ("s", "y", "x", "l", "h"))
    packed = jnp.concatenate(
        [medium_filters[0], short_filters[0].reshape(21, -1), norm_gain, jnp.zeros((10, 2 * HALF), BF16), out_weight[0]]
    )
    halves = packed[:, :HALF], packed[:, HALF:]
    mine = jnp.where(s == 0, halves[0], halves[1])
    theirs = other_core(jnp.where(s == 0, halves[1], halves[0]))
    layer_0 = jnp.where(s == 0, mine, theirs)
    layer_1 = jnp.where(s == 0, theirs, mine)
    own_ids = working_tokens(token_ids)
    before_ids = previous_tokens(token_ids[:, ROWS - HALO :])
    block_0 = (y == 0) & (l == 0) & (h == 0)
    before_ids = jnp.where(block_0, -1, before_ids)
    tokens = jnp.concatenate([before_ids, own_ids], axis=1)[:, :, None]
    table_half = lax.dynamic_slice_in_dim(embed_table, s * HALF, HALF, 1)
    message = jnp.concatenate([table_half, layer_0[:PAR], layer_1[:PAR]])
    part = message.shape[0] // 4
    quarter = lax.dynamic_slice_in_dim(message, y * part, part, 0)
    raw = jnp.concatenate([layer_0[PAR:], layer_1[PAR:]])
    first = from_block(jnp.concatenate([quarter, raw]), 0)
    shards = in_order([first[part:]] + [from_block(raw, by) for by in STEPS[1:]], x).reshape(4, 2, 64, HALF)
    message = in_order(ring(first[:part], "y"), y).reshape(4 * part, HALF)
    table, par_0, par_1 = message[:VOCAB], message[VOCAB : VOCAB + PAR], message[VOCAB + PAR :]
    where = jnp.stack([s, channel_block(x, l, h), l]).astype(jnp.int32)

    wide = embed_table.astype(F32)
    partial = jnp.sum(wide * wide, axis=1).reshape(4, 128)
    entry_scale = lax.rsqrt(sum(ring(partial, "h")) / D + 1e-06).reshape(VOCAB, 1)

    shards = after(shards, tokens, entry_scale)
    line_0 = line_weights(shards[:, 0])
    gated, stream = first_filters(after(tokens, shards), table, entry_scale, par_0)
    weights_0 = lax.all_gather(after(line_0, gated), "y")
    acts = gathered(gated)
    line_1 = line_weights(after(shards[:, 1], gated))
    stream_1, squares = project(where, acts, weights_0, after(stream, line_1))
    weights_1 = lax.all_gather(line_1, "y")

    halo = previous_block(stream_1.reshape(2, ROWS, HALF)[:, ROWS - HALO :])
    squares = lax.psum(squares.reshape(4, 128), ("s", "x"))
    scale = lax.rsqrt(squares.reshape(2, ROWS) / D + 1e-06)
    scale = jnp.concatenate([previous_block(scale[:, ROWS - HALO :]), scale], axis=1)[:, :, None]
    result_0a, result_0b = to_outputs_z(stream_1[:ROWS]), to_outputs_z(stream_1[ROWS:])
    gated = next_filters(stream_1, halo.reshape(2 * HALO, HALF), scale, par_1)
    acts = gathered(after(gated, result_0a), result_0b)
    stream_2, _ = project(where, acts, weights_1, stream_1)
    result_1 = to_outputs_x(to_outputs_z(stream_2))
    result_0 = to_outputs_x(jnp.concatenate([result_0a, result_0b]))

    kept = jnp.where(s == 0, result_0, result_1)
    received = other_core(jnp.where(s == 0, result_1, result_0))
    left = jnp.where(s == 0, kept, received)
    right = jnp.where(s == 0, received, kept)
    return jnp.concatenate([left, right], axis=1).reshape(1, 2, ROWS, 2 * HALF)


def solution(mesh):
    fine = Mesh(mesh.devices.reshape(2, 4, 4, 4, 4), ("s", "y", "x", "l", "h"))
    seq = ("y", "x", "l")
    in_specs = (
        P(None, seq),
        P(None, "h"),
        P("s", "h"),
        P("s", None, None, "h"),
        P("s", None, "h"),
        P("s", seq, "h"),
    )
    return jax.shard_map(local, mesh=fine, in_specs=in_specs, out_specs=P("s", None, seq, "h"), check_vma=False)
```

```python
import itertools

import jax
import jax.numpy as jnp
from jax import lax
from jax.experimental import pallas as pl
from jax.experimental.pallas import tpu as pltpu
from jax.sharding import Mesh, PartitionSpec as P

D = 4096
ROWS = 256
HALF = 512
HALO = 144
REACH = 128
TILE = 128
MED = 128
PAR = 160
VOCAB = 512
F32 = jnp.float32
BF16 = jnp.bfloat16


STEPS = (0, 1, 3, 2)
LINES = (0, 2, 1, 3)


def ring(value, axis):
    return [value] + [lax.ppermute(value, axis, [((i + by) % 4, i) for i in range(4)]) for by in STEPS[1:]]


def in_order(pieces, position):
    one, two, three = pieces[1], pieces[3], pieces[2]
    twice = jnp.stack([pieces[0], one, two, three, pieces[0], one, two])
    return lax.dynamic_slice_in_dim(twice, (4 - position) % 4, 4, 0)


def other_core(value):
    return lax.ppermute(value, "s", [(0, 1), (1, 0)])


def permuted(value, axes, source):
    pairs = []
    for target in itertools.product(range(4), repeat=len(axes)):
        index = [0, 0]
        for a, b in zip(source(*target), target):
            index = [index[0] * 4 + a % 4, index[1] * 4 + b]
        pairs.append(tuple(index))
    return lax.ppermute(value, axes, pairs)


def channel_block(x, l, h):
    return (x + h + l) % 4


def from_block(value):
    return permuted(value, ("x", "l", "h"), lambda x, l, h: (x, l, channel_block(x, l, h)))


def to_outputs_z(value):
    return permuted(value, ("x", "l", "h"), lambda x, l, h: (x, l, h - x - l))


def to_outputs_x(value):
    return permuted(value, ("x", "l", "h"), lambda x, l, h: (h - x - l, l, h))


def working_tokens(value):
    return permuted(value, ("x", "h"), lambda x, h: (h, x))


def previous_block(value):
    def index(r):
        y, x, z = r // 64, r // 16 % 4, r % 16
        return ((y * 4 + x) * 4 + z % 4) * 4 + z // 4

    pairs = []
    for y, z, x in itertools.product(range(4), range(16), range(4)):
        r = 16 * y + z
        if r:
            yp, zp = divmod(r - 1, 16)
            c = channel_block(x, z % 4, z // 4)
            xp = (c - zp // 4 - zp % 4) % 4
            pairs.append((index(64 * yp + 16 * xp + zp), index(64 * y + 16 * x + z)))
    return lax.ppermute(value, ("y", "x", "l", "h"), pairs)


def previous_tokens(value):
    pairs = []
    for r in range(1, 64):
        y, z = divmod(r, 16)
        yp, zp = divmod(r - 1, 16)
        for x in range(4):
            source = ((yp * 4 + zp // 4) * 4 + zp % 4) * 4 + x
            target = ((y * 4 + x) * 4 + z % 4) * 4 + z // 4
            pairs.append((source, target))
    return lax.ppermute(value, ("y", "x", "l", "h"), pairs)


def filters(normed, par, shifted, product, query, gated):
    taps = [[par[MED + 7 * f + s : MED + 7 * f + s + 1, :] for s in range(7)] for f in range(3)]
    step = 64
    for c in range((REACH + ROWS) // step):
        first = HALO - REACH + c * step
        own = c * step >= REACH
        sums = [None] * 3
        for s in range(7):
            window = normed[first - s : first - s + step, :]
            for f in range(3):
                if f or own:
                    term = taps[f][s] * window
                    sums[f] = term if sums[f] is None else sums[f] + term
        key = sums[1].astype(BF16).astype(F32)
        value = sums[2].astype(BF16).astype(F32)
        product[c * step : (c + 1) * step, :] = (key * value).astype(BF16).astype(F32)
        if own:
            query[c * step - REACH : (c + 1) * step - REACH, :] = sums[0].astype(BF16).astype(F32)
    for j in range(8):
        shifted[j, 8 : REACH + ROWS, :] = product[8 - j : REACH + ROWS - j, :]
    block = 128
    for c in range(ROWS // block):

        def taps8(a, total):
            eight = par[pl.ds(pl.multiple_of(8 * a, 8), 8), :]
            start = pl.multiple_of(c * block + REACH - 8 * a, 8)
            for j in range(8):
                total = total + eight[j : j + 1, :] * shifted[j, pl.ds(start, block), :]
            return total

        total = lax.fori_loop(0, REACH // 8, taps8, jnp.zeros((block, TILE), F32))
        rows = slice(c * block, (c + 1) * block)
        gated[rows, :] = (query[rows, :] * total).astype(BF16)


def first_kernel(tokens, table, scale, par_in, gated, stream, par, normed, shifted, product, query):
    par[...] = par_in[...].astype(F32)
    gain = par[MED + 21 : MED + 22, :]
    entries = (table[...].astype(F32) * scale[...] * gain).astype(BF16)
    ids = lax.broadcasted_iota(jnp.int32, (HALO + ROWS, VOCAB), 1)
    chosen = jnp.where(tokens[0] == ids, 1.0, 0.0).astype(BF16)
    both = jnp.concatenate([entries, table[...]], axis=1)
    picked = jnp.dot(chosen, both, preferred_element_type=F32)
    normed[...] = picked[:, :TILE]
    stream[...] = picked[HALO:, TILE:].astype(BF16)
    filters(normed, par, shifted, product, query, gated)


def next_kernel(own, halo, scale, par_in, gated, par, normed, shifted, product, query):
    par[...] = par_in[...].astype(F32)
    gain = par[MED + 21 : MED + 22, :]
    normed[:HALO, :] = (halo[...].astype(F32) * scale[0, :HALO] * gain).astype(BF16).astype(F32)
    normed[HALO:, :] = (own[...].astype(F32) * scale[0, HALO:] * gain).astype(BF16).astype(F32)
    filters(normed, par, shifted, product, query, gated)


def filter_scratch():
    return [
        pltpu.VMEM((PAR, TILE), F32),
        pltpu.VMEM((HALO + ROWS, TILE), F32),
        pltpu.VMEM((8, REACH + ROWS, TILE), F32),
        pltpu.VMEM((REACH + ROWS, TILE), F32),
        pltpu.VMEM((ROWS, TILE), F32),
    ]


SMALL = pl.CostEstimate(flops=1_000_000, bytes_accessed=1_000_000, transcendentals=0)
COST = pl.CostEstimate(flops=12_000_000_000, bytes_accessed=4_000_000, transcendentals=0)


def first_filters(tokens, table, scale, par):
    micros = tokens.shape[0]
    block = pl.BlockSpec((ROWS, TILE), lambda m, c: (m, c))
    return pl.pallas_call(
        first_kernel,
        grid=(micros, HALF // TILE),
        in_specs=[
            pl.BlockSpec((1, HALO + ROWS, 1), lambda m, c: (m, 0, 0)),
            pl.BlockSpec((VOCAB, TILE), lambda m, c: (0, c)),
            pl.BlockSpec((VOCAB, 1), lambda m, c: (0, 0)),
            pl.BlockSpec((PAR, TILE), lambda m, c: (0, c)),
        ],
        out_specs=[block, block],
        out_shape=[jax.ShapeDtypeStruct((micros * ROWS, HALF), BF16)] * 2,
        scratch_shapes=filter_scratch(),
        compiler_params=pltpu.CompilerParams(vmem_limit_bytes=32 * 1024 * 1024),
        cost_estimate=COST,
        name="first_filters",
    )(tokens, table, scale, par)


def next_filters(own, halo, scale, par):
    micros = scale.shape[0]
    return pl.pallas_call(
        next_kernel,
        grid=(micros, HALF // TILE),
        in_specs=[
            pl.BlockSpec((ROWS, TILE), lambda m, c: (m, c)),
            pl.BlockSpec((HALO, TILE), lambda m, c: (m, c)),
            pl.BlockSpec((1, HALO + ROWS, 1), lambda m, c: (m, 0, 0)),
            pl.BlockSpec((PAR, TILE), lambda m, c: (0, c)),
        ],
        out_specs=pl.BlockSpec((ROWS, TILE), lambda m, c: (m, c)),
        out_shape=jax.ShapeDtypeStruct((micros * ROWS, HALF), BF16),
        scratch_shapes=filter_scratch(),
        compiler_params=pltpu.CompilerParams(vmem_limit_bytes=32 * 1024 * 1024),
        cost_estimate=SMALL,
        name="next_filters",
    )(own, halo, scale, par)


def project_kernel(where, own, other, weights, stream, out, squares, whole, acts, sems, act_sems):
    s, c, l = where[0], where[1], where[2]
    copies = []
    for i in range(4):
        for j, flip in enumerate(LINES):
            copies.append(
                pltpu.make_async_copy(
                    weights.at[i, j], whole.at[i, :, lax.bitwise_xor(l, flip)], sems.at[i, j]
                )
            )
    copies.append(pltpu.make_async_copy(own, acts.at[0], act_sems.at[0]))
    copies.append(pltpu.make_async_copy(other, acts.at[1], act_sems.at[1]))
    for copy in copies:
        copy.start()
    for copy in copies:
        copy.wait()
    for m in range(stream.shape[0] // ROWS):
        rows = slice(m * ROWS, (m + 1) * ROWS)
        total = stream[rows, :].astype(F32)
        for i, step in enumerate(STEPS):
            for k in range(2):
                half = s if k == 0 else 1 - s
                w = whole[lax.rem(c + step, 4), pl.ds(2 * half, 2)].reshape(HALF, HALF)
                total = total + jnp.dot(acts[k, i, rows, :], w, preferred_element_type=F32)
        rounded = total.astype(BF16)
        out[rows, :] = rounded
        wide = rounded.astype(F32)
        squares[rows, :] = jnp.sum(wide * wide, axis=1, keepdims=True)


def project(where, acts, weights, stream):
    rows = stream.shape[0]
    vmem = pl.BlockSpec(memory_space=pltpu.VMEM)
    return pl.pallas_call(
        project_kernel,
        in_specs=[pl.BlockSpec(memory_space=pltpu.SMEM)] + [pl.BlockSpec(memory_space=pltpu.HBM)] * 3 + [vmem],
        out_specs=[vmem, vmem],
        out_shape=[
            jax.ShapeDtypeStruct((rows, HALF), BF16),
            jax.ShapeDtypeStruct((rows, 1), F32),
        ],
        scratch_shapes=[
            pltpu.VMEM((4, 4, 4, 64, HALF), BF16),
            pltpu.VMEM((2, 4, rows, HALF), BF16),
            pltpu.SemaphoreType.DMA((4, 4)),
            pltpu.SemaphoreType.DMA((2,)),
        ],
        compiler_params=pltpu.CompilerParams(vmem_limit_bytes=40 * 1024 * 1024),
        cost_estimate=pl.CostEstimate(flops=4_000_000_000, bytes_accessed=9_000_000, transcendentals=0),
        name="project",
    )(where, *acts, weights, stream)


def after(value, *others):
    return lax.optimization_barrier((value, *others))[0]


def gathered(gated, *others):
    own = jnp.stack(ring(gated, "x"))
    return own, other_core(after(own, *others))


def line_weights(shard):
    pieces = [shard]
    for flip in LINES[1:]:
        pieces.append(permuted(shard, ("x", "l"), lambda x, l, flip=flip: (x + l - (l ^ flip), l ^ flip)))
    return jnp.stack(pieces)


def local(token_ids, embed_table, norm_gain, short_filters, medium_filters, out_weight):
    s, y, x, l, h = (lax.axis_index(a) for a in ("s", "y", "x", "l", "h"))
    packed = jnp.concatenate(
        [medium_filters[0], short_filters[0].reshape(21, -1), norm_gain, jnp.zeros((10, 2 * HALF), BF16), out_weight[0]]
    )
    halves = packed[:, :HALF], packed[:, HALF:]
    mine = jnp.where(s == 0, halves[0], halves[1])
    theirs = other_core(jnp.where(s == 0, halves[1], halves[0]))
    layer_0 = jnp.where(s == 0, mine, theirs)
    layer_1 = jnp.where(s == 0, theirs, mine)
    own_ids = working_tokens(token_ids)
    before_ids = previous_tokens(token_ids[:, ROWS - HALO :])
    block_0 = (y == 0) & (l == 0) & (h == 0)
    before_ids = jnp.where(block_0, -1, before_ids)
    tokens = jnp.concatenate([before_ids, own_ids], axis=1)[:, :, None]
    table_half = lax.dynamic_slice_in_dim(embed_table, s * HALF, HALF, 1)
    message = jnp.concatenate([table_half, layer_0[:PAR], layer_1[:PAR]])
    part = message.shape[0] // 4
    quarter = lax.dynamic_slice_in_dim(message, y * part, part, 0)
    first = from_block(quarter)
    message = in_order(ring(first, "y"), y).reshape(4 * part, HALF)
    shards = lax.all_gather(jnp.stack([layer_0[PAR:], layer_1[PAR:]]), "x")
    shards = from_block(shards.reshape(8 * 64, HALF)).reshape(4, 2, 64, HALF)
    table, par_0, par_1 = message[:VOCAB], message[VOCAB : VOCAB + PAR], message[VOCAB + PAR :]
    where = jnp.stack([s, channel_block(x, l, h), l]).astype(jnp.int32)

    wide = embed_table.astype(F32)
    partial = jnp.sum(wide * wide, axis=1).reshape(4, 128)
    entry_scale = lax.rsqrt(sum(ring(partial, "h")) / D + 1e-06).reshape(VOCAB, 1)

    gated, stream = first_filters(tokens, table, entry_scale, par_0)
    line_0 = line_weights(after(shards[:, 0], gated))
    weights_0 = lax.all_gather(line_0, "y")
    acts = gathered(gated)
    line_1 = line_weights(after(shards[:, 1], gated))
    stream_1, squares = project(where, acts, weights_0, after(stream, line_1))
    weights_1 = lax.all_gather(line_1, "y")

    halo = previous_block(stream_1.reshape(2, ROWS, HALF)[:, ROWS - HALO :])
    squares = lax.psum(squares.reshape(4, 128), ("s", "x"))
    scale = lax.rsqrt(squares.reshape(2, ROWS) / D + 1e-06)
    scale = jnp.concatenate([previous_block(scale[:, ROWS - HALO :]), scale], axis=1)[:, :, None]
    result_0a, result_0b = to_outputs_z(stream_1[:ROWS]), to_outputs_z(stream_1[ROWS:])
    gated = next_filters(stream_1, halo.reshape(2 * HALO, HALF), scale, par_1)
    acts = gathered(after(gated, result_0a), result_0b)
    stream_2, _ = project(where, acts, weights_1, stream_1)
    result_1 = to_outputs_x(to_outputs_z(stream_2))
    result_0 = to_outputs_x(jnp.concatenate([result_0a, result_0b]))

    kept = jnp.where(s == 0, result_0, result_1)
    received = other_core(jnp.where(s == 0, result_1, result_0))
    left = jnp.where(s == 0, kept, received)
    right = jnp.where(s == 0, received, kept)
    return jnp.concatenate([left, right], axis=1).reshape(1, 2, ROWS, 2 * HALF)


def solution(mesh):
    fine = Mesh(mesh.devices.reshape(2, 4, 4, 4, 4), ("s", "y", "x", "l", "h"))
    seq = ("y", "x", "l")
    in_specs = (
        P(None, seq),
        P(None, "h"),
        P("s", "h"),
        P("s", None, None, "h"),
        P("s", None, "h"),
        P("s", seq, "h"),
    )
    return jax.shard_map(local, mesh=fine, in_specs=in_specs, out_specs=P("s", None, seq, "h"), check_vma=False)
```
